32 devices in a mesh: groups: 2 (over y), mp: 4 (over x, core), dp: 4 (over z).
Axes of the slice: x: 2, y: 2, z: 4, core: 2. Of those that a mesh axis runs over, the one named last changes fastest.
Arguments:
- qkv: bfloat16 [3, 8192, 4096], P(None, ('groups', 'dp'), 'mp'), parts along dimension 1, may hold values from -6.5 to 6.5
- grad_out: float32 [8192, 6144], P(('groups', 'dp'), 'mp'), parts along dimension 0, may hold values from -6 to 6
- out_weight: bfloat16 [4096, 6144], P('mp', 'dp'), may hold values from -0.09375 to 0.09375
- segments: int32 [16, 512], P(('groups', 'dp')), parts along dimension 0, may hold values from 0 to 15, as said below
Outputs:
- grad_qkv: bfloat16 [3, 8192, 4096], P(None, ('groups', 'dp'), 'mp'), parts along dimension 1
- grad_weight: bfloat16 [8192, 6144], P(('groups', 'mp'), 'dp'), parts along dimension 0
The draws below stay inside these ranges and needn't reach their ends.
There are 2 independent parts, one for each index of `groups`. The reference program is written for one: setup_inputs(seed, part) draws one part's arguments, and reference() takes and returns one part's arrays. A program takes and returns all parts, laid end to end along the dimension named above; an argument that names none is the same for every part. Nothing has to cross between parts.
Inputs may be any that keep to these rules, and one draw needn't show every extreme that they name: `segments`: along each packed sequence the image ids start at 0 and never fall; every image covers a run of even length that starts at an even position.
All inputs are finite; a program needn't handle non-finite values.
Results may differ from the reference program's by a relative error of at most 0.0075.
Values may be sent and summed in bfloat16 or wider, within the bound.
No kernel may reach another device: no remote copies, remote signals or barrier semaphores. Data moves between devices by JAX's collectives and lax.ppermute only.
A program may use at most 256 MiB of HBM per device.

```python
import math
import jax
import jax.numpy as jnp
from jax import lax

D = 6144
HEADS = 32
HD = 128
LEN = 512
TOKENS = 4096
SEQS = 8


def draw_qkv(key, part):
    key = jax.random.fold_in(key, 11)
    keys_list = jax.random.split(key, 1)
    width = HEADS * HD
    base = jax.random.normal(keys_list[0], (3, TOKENS, width), jnp.float32)
    return jnp.clip(base, -6.0, 6.0).astype(jnp.bfloat16)


def draw_segments(key, part):
    key = jax.random.fold_in(key, 23)
    keys_list = jax.random.split(key, 3)
    half = LEN // 2
    order = jax.vmap(lambda sub: jax.random.permutation(sub, half - 1))(jax.random.split(keys_list[0], SEQS))
    cuts_count = jax.random.randint(keys_list[1], (SEQS, 1), 1, 16)
    forced = jax.random.randint(keys_list[2], (), 0, SEQS)
    cuts_count = jnp.where(jnp.arange(SEQS)[:, None] == forced, 15, cuts_count)
    is_cut = (order < cuts_count).astype(jnp.int32)
    halves = jnp.concatenate([jnp.zeros((SEQS, 1), jnp.int32), jnp.cumsum(is_cut, axis=1).astype(jnp.int32)], axis=1)
    return jnp.repeat(halves, 2, axis=1).astype(jnp.int32)


def spiked(entries, rng, source, target, blocks, factor):
    def block_of(axis_at):
        return (jnp.arange(entries.shape[axis_at]) // (entries.shape[axis_at] // blocks)).reshape((-1,) + (1,) * (entries.ndim - 1 - axis_at))

    one_side = jax.random.permutation(rng, blocks)[block_of(target)]
    second = (block_of(target) + blocks // 2) % blocks
    return jnp.where((block_of(source) == one_side) | (block_of(source) == second), factor * entries, entries)


def block_scale(stream_key, shape, cuts, least, top_value):
    factor_of = 1.0
    for dim, parts in cuts:
        heights = jax.random.uniform(jax.random.fold_in(jax.random.fold_in(stream_key, 6), dim), (parts,), jnp.float32, least / len(cuts), top_value / len(cuts))
        factor_of = factor_of * jnp.repeat(jnp.exp(heights), shape[dim] // parts).reshape((-1,) + (1,) * (len(shape) - 1 - dim))
    return factor_of


def scatter_about(stream_key, shape, spread, limit, cuts=(), kind=jnp.bfloat16):
    level = block_scale(stream_key, shape, cuts, -0.22, 0.18) if cuts else 1.0
    values = jax.random.normal(stream_key, shape, jnp.float32) * spread * level
    return jnp.minimum(jnp.maximum(values, -limit), limit).astype(kind)


def heavy_noise(rng, shape, spread, limit, pieces, heavy, held_as=jnp.bfloat16):
    entries = spread * jax.random.normal(rng, shape, jnp.float32)
    if pieces:
        entries = entries * block_scale(rng, shape, pieces, -0.22, 0.18)
    return jnp.clip(spiked(entries, jax.random.fold_in(rng, 3), *heavy), -limit, limit).astype(held_as)


def setup_inputs(seed: int = 0, part: int = 0) -> dict:
    arg_keys = jax.random.split(jax.random.key(seed), 5)
    part_keys = jax.random.split(jax.random.fold_in(arg_keys[4], part), 5)
    qkv = draw_qkv(jax.random.fold_in(jax.random.fold_in(arg_keys[4], part), 71), part)
    grad_out = heavy_noise(part_keys[1], (TOKENS, D), 1.0, 6.0, ((0, 4), (1, 4)), (0, 1, 4, 2.0), jnp.float32)
    out_weight = scatter_about(arg_keys[2], (HEADS * HD, D), (HEADS * HD) ** -0.5, 0.09375, ((0, 4), (1, 4)))
    segments = draw_segments(jax.random.fold_in(jax.random.fold_in(arg_keys[4], part), 71), part)
    return dict(qkv=qkv, grad_out=grad_out, out_weight=out_weight, segments=segments)


def masked_softmax(scores, allowed):
    scores = jnp.where(allowed[None], scores, -jnp.inf)
    row_max = lax.optimization_barrier(jnp.max(scores, axis=-1, keepdims=True))
    exponent = jnp.exp(scores - row_max)
    return exponent / lax.optimization_barrier(jnp.sum(exponent, axis=-1, keepdims=True))

def sequence_probability(queries, keys, segment_ids):
    allowed = segment_ids[:, None] == segment_ids[None, :]
    scores = jnp.einsum('qhd,khd->hqk', queries.astype(jnp.float32), keys.astype(jnp.float32))
    scores = scores * (1.0 / math.sqrt(HD))
    return masked_softmax(scores, allowed)

def reference(qkv, grad_out, out_weight, segments):
    count = TOKENS // LEN
    width = HEADS * HD
    shaped = qkv.reshape(3, count, LEN, HEADS, HD)

    def forward(bundle):
        queries, keys, values, segment_ids = bundle
        probability = sequence_probability(queries, keys, segment_ids)
        weights = probability.astype(jnp.bfloat16)
        return jnp.einsum('hqk,khd->qhd', weights.astype(jnp.float32), values.astype(jnp.float32)).astype(jnp.bfloat16)
    attended = lax.map(forward, (shaped[0], shaped[1], shaped[2], segments))
    attended_rows = attended.reshape(TOKENS, width)
    grad_rows = grad_out.astype(jnp.bfloat16)
    grad_attended = jnp.dot(grad_rows, out_weight.T, preferred_element_type=jnp.float32).astype(jnp.bfloat16)
    grad_weight = jnp.dot(attended_rows.T, grad_rows, preferred_element_type=jnp.float32).astype(jnp.bfloat16)
    grad_heads = grad_attended.reshape(count, LEN, HEADS, HD)

    def backward(bundle):
        queries, keys, values, segment_ids, grad_att = bundle
        probability = sequence_probability(queries, keys, segment_ids)
        weights = probability.astype(jnp.bfloat16)
        grad_probs = jnp.einsum('qhd,khd->hqk', grad_att.astype(jnp.float32), values.astype(jnp.float32))
        row_dot = lax.optimization_barrier(jnp.sum(probability * grad_probs, axis=-1, keepdims=True))
        grad_scores = (probability * (grad_probs - row_dot) * (1.0 / math.sqrt(HD))).astype(jnp.bfloat16)
        grad_queries = jnp.einsum('hqk,khd->qhd', grad_scores.astype(jnp.float32), keys.astype(jnp.float32))
        grad_keys = jnp.einsum('hqk,qhd->khd', grad_scores.astype(jnp.float32), queries.astype(jnp.float32))
        grad_values = jnp.einsum('hqk,qhd->khd', weights.astype(jnp.float32), grad_att.astype(jnp.float32))
        return jnp.stack([grad_queries, grad_keys, grad_values]).astype(jnp.bfloat16)
    grads = lax.map(backward, (shaped[0], shaped[1], shaped[2], segments, grad_heads))
    grad_qkv = jnp.transpose(grads, (1, 0, 2, 3, 4)).reshape(3, TOKENS, width)
    return (grad_qkv, grad_weight)
```

```python
import functools
import math

import jax
import jax.numpy as jnp
from jax import lax
from jax.experimental import pallas as pl
from jax.experimental.pallas import tpu as pltpu
from jax.sharding import PartitionSpec as P

HD = 128
LEN = 512
SCALE = 1.0 / math.sqrt(HD)
CHUNKS = 4
NT = (((1,), (1,)), ((), ()))
NN = (((1,), (0,)), ((), ()))
TN = (((0,), (0,)), ((), ()))


def dot(a, b, dims):
    return lax.dot_general(a, b, dims, preferred_element_type=jnp.float32)


def probabilities(queries, keys, allowed):
    scores = jnp.where(allowed, dot(queries, keys, NT) * SCALE, -jnp.inf)
    exponent = jnp.exp(scores - jnp.max(scores, axis=-1, keepdims=True))
    return exponent * (1.0 / jnp.sum(exponent, axis=-1, keepdims=True))


def forward_kernel(column_ids, row_ids, qkv, attended):
    allowed = column_ids[0] == row_ids[0]
    for head in range(attended.shape[1] // HD):
        cols = slice(head * HD, (head + 1) * HD)
        weights = probabilities(qkv[0, :, cols], qkv[1, :, cols], allowed).astype(jnp.bfloat16)
        attended[:, cols] = dot(weights, qkv[2, :, cols], NN).astype(jnp.bfloat16)


def backward_kernel(column_ids, row_ids, qkv, grad_att, grad_qkv):
    allowed = column_ids[0] == row_ids[0]
    for head in range(grad_att.shape[1] // HD):
        cols = slice(head * HD, (head + 1) * HD)
        queries, keys, values = qkv[0, :, cols], qkv[1, :, cols], qkv[2, :, cols]
        grads = grad_att[:, cols]
        probability = probabilities(queries, keys, allowed)
        grad_probs = dot(grads, values, NT)
        row_dot = jnp.sum(probability * grad_probs, axis=-1, keepdims=True)
        grad_scores = (probability * (grad_probs - row_dot) * SCALE).astype(jnp.bfloat16)
        weights = probability.astype(jnp.bfloat16)
        grad_qkv[0, :, cols] = dot(grad_scores, keys, NN).astype(jnp.bfloat16)
        grad_qkv[1, :, cols] = dot(grad_scores, queries, TN).astype(jnp.bfloat16)
        grad_qkv[2, :, cols] = dot(weights, grads, TN).astype(jnp.bfloat16)


def attention_call(kernel, segments, qkv, grad_att=None):
    tokens, width = qkv.shape[1:]
    seqs = tokens // LEN
    block = 2 * HD
    rows = pl.BlockSpec((LEN, block), lambda s, h: (s, h))
    three = pl.BlockSpec((3, LEN, block), lambda s, h: (0, s, h))
    in_specs = [
        pl.BlockSpec((1, LEN, 1), lambda s, h: (s, 0, 0)),
        pl.BlockSpec((1, 1, LEN), lambda s, h: (s, 0, 0)),
        three,
    ]
    operands = [segments.reshape(seqs, LEN, 1), segments.reshape(seqs, 1, LEN), qkv]
    out_specs, out_shape, products = rows, (tokens, width), 2
    if grad_att is not None:
        in_specs.append(rows)
        operands.append(grad_att)
        out_specs, out_shape, products = three, qkv.shape, 5
    return pl.pallas_call(
        kernel,
        grid=(seqs, width // block),
        in_specs=in_specs,
        out_specs=out_specs,
        out_shape=jax.ShapeDtypeStruct(out_shape, jnp.bfloat16),
        compiler_params=pltpu.CompilerParams(vmem_limit_bytes=48 * 2**20),
        cost_estimate=pl.CostEstimate(
            flops=2 * products * tokens * LEN * width,
            bytes_accessed=2 * products * 2 * tokens * width,
            transcendentals=tokens * LEN * width // HD,
        ),
    )(*operands)


def shards(groups, mp, dp, qkv, grad_out, out_weight, segments):
    tokens, width = qkv.shape[1:]
    own_width = grad_out.shape[1]
    per = mp // dp
    group = lax.axis_index("groups")
    here = lax.axis_index("mp")
    place = lax.axis_index("dp")

    def along(array, pairs):
        return lax.ppermute(array, "dp", pairs)

    def across_groups(array, shift, places):
        pairs = [
            (g * dp + k, (g + shift) % groups * dp + k) for g in range(groups) for k in places
        ]
        return lax.ppermute(array, ("groups", "dp"), pairs)

    with jax.named_scope("projection_along_dp"):
        part_rows = width // groups
        own_part = lax.dynamic_slice_in_dim(out_weight, group * part_rows, part_rows, 0)
        rights, lefts = [], []
        to_right = to_left = own_part
        for step in range(dp - 1):
            to_right = along(to_right, [(k, k + 1) for k in range(step, dp - 1)])
            to_left = along(to_left, [(k, k - 1) for k in range(1, dp - step)])
            rights.append(to_right)
            lefts.append(to_left)

    attended = attention_call(forward_kernel, segments, qkv)

    with jax.named_scope("output_gradient_over_mp"):
        chunk = own_width // CHUNKS
        gathered = []
        for c in range(CHUNKS):
            mine = grad_out[:, c * chunk : (c + 1) * chunk].astype(jnp.bfloat16)
            blocks = {0: mine}
            bit = mp // 2
            while bit:
                pairs = [(i, i ^ bit) for i in range(mp)]
                blocks |= {at | bit: lax.ppermute(b, "mp", pairs) for at, b in blocks.items()}
                bit //= 2
            gathered.append(jnp.stack([blocks[at] for at in range(mp)]))

    with jax.named_scope("weight_gradient_partials"):
        partials = [
            lax.dot_general(
                gathered[c],
                attended,
                (((1,), (0,)), ((), ())),
                preferred_element_type=jnp.float32,
            )
            for c in range(CHUNKS)
        ]

    def pick(stacked, which, axis):
        found = [
            lax.dynamic_index_in_dim(stacked, (which * per + j) ^ here, 0, keepdims=False)
            for j in range(per)
        ]
        return found[0] if per == 1 else jnp.concatenate(found, axis=axis)

    with jax.named_scope("weight_gradient_along_dp"):
        from_left = [None] * CHUNKS
        from_right = [None] * CHUNKS
        for step in range(dp - 1):
            for c in range(CHUNKS):
                right = pick(partials[c], jnp.minimum(dp - 1 - step + place, dp - 1), 0)
                left = pick(partials[c], jnp.maximum(step - dp + 1 + place, 0), 0)
                if step:
                    right = right + from_left[c].astype(jnp.float32)
                    left = left + from_right[c].astype(jnp.float32)
                from_left[c] = along(
                    right.astype(jnp.bfloat16),
                    [(k, k + 1) for k in range(min(step + 1, dp - 1))],
                )
                from_right[c] = along(
                    left.astype(jnp.bfloat16),
                    [(k, k - 1) for k in range(max(dp - 1 - step, 1), dp)],
                )
        sums = []
        for c in range(CHUNKS):
            total = pick(partials[c], place, 0)
            total = total + from_left[c].astype(jnp.float32) + from_right[c].astype(jnp.float32)
            sums.append(total.astype(jnp.bfloat16).T.reshape(width, per, chunk))
        grad_weight = jnp.stack(sums, axis=2).reshape(width, per * own_width)

    with jax.named_scope("attended_gradient"):
        whole = jnp.concatenate(gathered, axis=2)

        def product(which, parts):
            features = pick(whole, which, 1)
            return dot(features, jnp.concatenate(parts, axis=0), NT)

        own_parts = [
            lax.dynamic_slice_in_dim(
                out_weight, (group + j) % groups * part_rows, part_rows, 0
            )
            for j in range(groups)
        ]
        total = product(place, own_parts)
        for step in range(dp - 1):
            back = dp - 2 - step
            parts = [rights[step] + lefts[back]]
            for j in range(1, groups):
                parts.append(
                    across_groups(rights[step], -j, range(step + 1, dp))
                    + across_groups(lefts[back], -j, range(0, dp - 1 - back))
                )
            total = total + product((place - 1 - step) % dp, parts)
        rounded = total.astype(jnp.bfloat16)
        grad_att = jnp.roll(rounded, group * part_rows, axis=1)

    grad_qkv = attention_call(backward_kernel, segments, qkv, grad_att)
    return grad_qkv, grad_weight


def solution(mesh):
    body = functools.partial(shards, *(mesh.shape[name] for name in ("groups", "mp", "dp")))
    return jax.shard_map(
        body,
        mesh=mesh,
        in_specs=(
            P(None, ("groups", "dp"), "mp"),
            P(("groups", "dp"), "mp"),
            P("mp", "dp"),
            P(("groups", "dp"), None),
        ),
        out_specs=(P(None, ("groups", "dp"), "mp"), P(("groups", "mp"), "dp")),
        check_vma=False,
    )
```

```python
import functools
import math

import jax
import jax.numpy as jnp
from jax import lax
from jax.experimental import pallas as pl
from jax.experimental.pallas import tpu as pltpu
from jax.sharding import PartitionSpec as P

HD = 128
LEN = 512
SCALE = 1.0 / math.sqrt(HD)
CHUNKS = 3
LIGHT = 20
NT = (((1,), (1,)), ((), ()))
NN = (((1,), (0,)), ((), ()))
TN = (((0,), (0,)), ((), ()))
ROOM = pltpu.CompilerParams(vmem_limit_bytes=48 * 2**20)


def dot(a, b, dims):
    return lax.dot_general(a, b, dims, preferred_element_type=jnp.float32)


def cost(flops, moved):
    return pl.CostEstimate(flops=flops // LIGHT, bytes_accessed=moved // LIGHT, transcendentals=0)


def after(array, *others):
    return lax.optimization_barrier((array, *others))[0]


def probabilities(queries, keys, allowed):
    scores = jnp.where(allowed, dot(queries, keys, NT) * SCALE, -jnp.inf)
    exponent = jnp.exp(scores - jnp.max(scores, axis=-1, keepdims=True))
    return exponent * (1.0 / jnp.sum(exponent, axis=-1, keepdims=True))


def forward_kernel(column_ids, row_ids, qkv, attended):
    allowed = column_ids[0] == row_ids[0]
    for head in range(attended.shape[0] // HD):
        cols = slice(head * HD, (head + 1) * HD)
        weights = probabilities(qkv[0, :, cols], qkv[1, :, cols], allowed).astype(jnp.bfloat16)
        attended[cols, :] = dot(weights, qkv[2, :, cols], NN).astype(jnp.bfloat16).T


def backward_kernel(column_ids, row_ids, qkv, grad_att, *refs):
    grad_qkv = refs[-1]
    allowed = column_ids[0] == row_ids[0]
    for head in range(grad_att.shape[1] // HD):
        cols = slice(head * HD, (head + 1) * HD)
        queries, keys, values = qkv[0, :, cols], qkv[1, :, cols], qkv[2, :, cols]
        grads = grad_att[:, cols]
        probability = probabilities(queries, keys, allowed)
        grad_probs = dot(grads, values, NT)
        row_dot = jnp.sum(probability * grad_probs, axis=-1, keepdims=True)
        grad_scores = (probability * (grad_probs - row_dot) * SCALE).astype(jnp.bfloat16)
        weights = probability.astype(jnp.bfloat16)
        grad_qkv[0, :, cols] = dot(grad_scores, keys, NN).astype(jnp.bfloat16)
        grad_qkv[1, :, cols] = dot(grad_scores, queries, TN).astype(jnp.bfloat16)
        grad_qkv[2, :, cols] = dot(weights, grads, TN).astype(jnp.bfloat16)


def attention_specs(segments, qkv, start):
    seqs = qkv.shape[1] // LEN
    block = 2 * HD
    three = pl.BlockSpec((3, LEN, block), lambda s, h: (0, start + s, h))
    in_specs = [
        pl.BlockSpec((1, LEN, 1), lambda s, h: (start + s, 0, 0)),
        pl.BlockSpec((1, 1, LEN), lambda s, h: (start + s, 0, 0)),
        three,
    ]
    return in_specs, [segments.reshape(seqs, LEN, 1), segments.reshape(seqs, 1, LEN), qkv]


def attention_forward(segments, qkv):
    tokens, width = qkv.shape[1:]
    block = 2 * HD
    in_specs, operands = attention_specs(segments, qkv, 0)
    return pl.pallas_call(
        forward_kernel,
        grid=(tokens // LEN, width // block),
        in_specs=in_specs,
        out_specs=pl.BlockSpec((block, LEN), lambda s, h: (h, s)),
        out_shape=jax.ShapeDtypeStruct((width, tokens), jnp.bfloat16),
        compiler_params=ROOM,
        cost_estimate=cost(2 * 2 * tokens * LEN * width, 8 * tokens * width),
    )(*operands)


def attention_backward(segments, qkv, grad_att, start, into):
    tokens, width = qkv.shape[1:]
    block = 2 * HD
    rows = grad_att.shape[0]
    in_specs, operands = attention_specs(segments, qkv, start)
    in_specs.append(pl.BlockSpec((LEN, block), lambda s, h: (s, h)))
    operands.append(grad_att)
    if into is not None:
        in_specs.append(pl.BlockSpec(memory_space=pl.ANY))
        operands.append(into)
    return pl.pallas_call(
        backward_kernel,
        grid=(rows // LEN, width // block),
        in_specs=in_specs,
        out_specs=in_specs[2],
        out_shape=jax.ShapeDtypeStruct(qkv.shape, jnp.bfloat16),
        input_output_aliases={} if into is None else {4: 0},
        compiler_params=ROOM,
        cost_estimate=cost(2 * 5 * rows * LEN * width, 14 * rows * width),
    )(*operands)


def partial_kernel(order, attended, *refs):
    *features, pair, third, own, held = refs
    for at, block in enumerate(features):
        held[at] = dot(attended[...], block[...], NN)
    for at, out in enumerate((pair.at[0], pair.at[1], third, own)):
        out[...] = held[order[at]].astype(out.dtype)


def partial_call(order, attended, features):
    width, tokens = attended.shape
    chunk = features[0].shape[1]
    rows = min(256, width)
    out = pl.BlockSpec((rows, chunk), lambda r, _: (r, 0))
    return pl.pallas_call(
        partial_kernel,
        grid_spec=pltpu.PrefetchScalarGridSpec(
            num_scalar_prefetch=1,
            grid=(width // rows,),
            in_specs=[pl.BlockSpec((rows, tokens), lambda r, _: (r, 0))]
            + [pl.BlockSpec((tokens, chunk), lambda r, _: (0, 0)) for _ in features],
            out_specs=[pl.BlockSpec((2, rows, chunk), lambda r, _: (0, r, 0)), out, out],
            scratch_shapes=[pltpu.VMEM((len(features), rows, chunk), jnp.float32)],
        ),
        out_shape=[
            jax.ShapeDtypeStruct((2, width, chunk), jnp.bfloat16),
            jax.ShapeDtypeStruct((width, chunk), jnp.bfloat16),
            jax.ShapeDtypeStruct((width, chunk), jnp.float32),
        ],
        compiler_params=ROOM,
        cost_estimate=cost(
            2 * len(features) * chunk * width * tokens,
            2 * len(features) * chunk * (tokens + width) + 2 * width * tokens,
        ),
    )(order, attended, *features)


def attended_kernel(order, *refs):
    *features, own, one, one_far, two, two_far, three, three_far, out, held = refs
    blocks = held.shape[0]
    pieces = len(features) // blocks
    half = one.shape[0]
    for at in range(blocks):
        start = 0
        for piece in features[at * pieces : (at + 1) * pieces]:
            stop = start + piece.shape[1]
            held[at, :, start:stop] = piece[...]
            start = stop
    near_start = pl.multiple_of(order[4] * half, HD)
    far_start = pl.multiple_of((1 - order[4]) * half, HD)
    near = dot(held[order[0]], own[pl.ds(near_start, half), :], NT)
    far = dot(held[order[0]], own[pl.ds(far_start, half), :], NT)
    for slot, (here, there) in enumerate(((one, one_far), (two, two_far), (three, three_far))):
        near += dot(held[order[slot + 1]], here[...], NT)
        far += dot(held[order[slot + 1]], there[...], NT)
    out[:, pl.ds(near_start, half)] = near.astype(jnp.bfloat16)
    out[:, pl.ds(far_start, half)] = far.astype(jnp.bfloat16)


def attended_call(order, gathered, weights, start, tokens):
    width, own_width = weights[0].shape
    blocks = len(gathered[0])
    features = [pieces[at] for at in range(blocks) for pieces in gathered]
    rows = min(256, tokens)
    skip = start // rows
    return pl.pallas_call(
        attended_kernel,
        grid_spec=pltpu.PrefetchScalarGridSpec(
            num_scalar_prefetch=1,
            grid=(tokens // rows,),
            in_specs=[pl.BlockSpec((rows, f.shape[1]), lambda r, _: (skip + r, 0)) for f in features]
            + [
                pl.BlockSpec(w.shape, lambda r, _: (0, 0), pipeline_mode=pl.Buffered(1))
                for w in weights
            ],
            out_specs=pl.BlockSpec((rows, width), lambda r, _: (r, 0)),
            scratch_shapes=[pltpu.VMEM((blocks, rows, own_width), jnp.bfloat16)],
        ),
        out_shape=jax.ShapeDtypeStruct((tokens, width), jnp.bfloat16),
        compiler_params=ROOM,
        cost_estimate=cost(
            2 * tokens * width * blocks * own_width,
            2 * (blocks * own_width * (tokens + width) + tokens * width),
        ),
    )(order, *features, *weights)


def plain_shards(qkv, grad_out, out_weight, segments):
    attended = attention_forward(segments, qkv)
    rows = lax.all_gather(grad_out.astype(jnp.bfloat16), "mp", axis=1, tiled=True)
    projection = lax.all_gather(out_weight, "dp", axis=1, tiled=True)
    block = dot(attended, rows, NN)
    grad_weight = lax.psum_scatter(block, "dp", scatter_dimension=1, tiled=True)
    grad_att = dot(rows, projection, NT).astype(jnp.bfloat16)
    grad_qkv = attention_backward(segments, qkv, grad_att, 0, None)
    return grad_qkv, grad_weight.astype(jnp.bfloat16)


OUTER = [(0, 1), (1, 0), (2, 3), (3, 2)]
INWARD = [(0, 1), (3, 2)]
MIDDLE = [(1, 2), (2, 1)]
OUTWARD = [(1, 0), (2, 3)]


def shards(qkv, grad_out, out_weight, segments):
    width = qkv.shape[2]
    own_width = grad_out.shape[1]
    chunk = own_width // CHUNKS
    group = lax.axis_index("groups")
    here = lax.axis_index("mp")
    place = lax.axis_index("dp")
    outer = (place == 0) | (place == 3)
    low = place < 2

    def along(array, pairs):
        return lax.ppermute(array, "dp", pairs)

    def swap_groups(array):
        return lax.ppermute(array, "groups", [(0, 1), (1, 0)])

    last = []

    def chained(array, *others):
        return after(array, *last, *others)

    def done(*arrays):
        last[:] = arrays[:1]
        return arrays[0] if len(arrays) == 1 else arrays

    half = width // 2
    own_half = lax.dynamic_slice_in_dim(out_weight, group * half, half, 0)
    first = along(own_half, OUTER)
    middle = along(own_half, MIDDLE)
    first_far = swap_groups(first)
    middle_second = along(first, MIDDLE)
    outward = along(middle, OUTWARD)
    outward_second = along(middle_second, OUTWARD)

    attended = done(attention_forward(segments, qkv))

    partial_order = jnp.stack(
        [
            jnp.where(low, 3, 0) ^ here,
            jnp.where(low, 2, 1) ^ here,
            jnp.where(outer, jnp.where(low, 1, 2), jnp.where(low, 0, 3)) ^ here,
            place ^ here,
        ]
    ).astype(jnp.int32)
    gathered, partials = [], []

    def gather(c):
        mine = grad_out[:, c * chunk : (c + 1) * chunk].astype(jnp.bfloat16)
        if c:
            mine = after(mine, attended)
        near = lax.ppermute(mine, "mp", [(i, i ^ 1) for i in range(4)])
        across = lax.ppermute(mine, "mp", [(i, i ^ 2) for i in range(4)])
        both = lax.ppermute(chained(across), "mp", [(i, i ^ 1) for i in range(4)])
        gathered.append([mine, near, across, both])

    def partial(c, *others):
        partials.append(
            done(*partial_call(chained(partial_order, *others), attended, gathered[c]))
        )

    pairs_in, last_in, middle_sums, outward_sums = [], [], [], []

    def send_pair(c, *others):
        value = partials[c][0]
        if others:
            value = after(value, *others)
        pairs_in.append(along(value, INWARD))

    def send_last(c, *others):
        last_in.append(along(after(partials[c][1], *others), INWARD))

    def send_middle(t, c, *others):
        mine, arrived = chained(partials[c][0], *others)[t], pairs_in[c][t]
        value = mine.astype(jnp.float32) + arrived.astype(jnp.float32)
        middle_sums.append(along(done(value.astype(jnp.bfloat16)), MIDDLE))

    def send_outward(c, *others):
        arrived = middle_sums[2 * c]
        value = chained(partials[c][1], *others).astype(jnp.float32)
        value = value + arrived.astype(jnp.float32)
        outward_sums.append(along(done(value.astype(jnp.bfloat16)), OUTWARD))

    grads = [None]
    attended_order = jnp.stack(
        [
            place ^ here,
            (place ^ 1) ^ here,
            jnp.where(low, 2, 1) ^ here,
            jnp.where(low, 3, 0) ^ here,
            group,
        ]
    ).astype(jnp.int32)
    grad_att = []

    def attended_gradient(s, *others):
        weights = [out_weight, first, first_far, second, second_far, third, third_far]
        found = attended_call(chained(attended_order, *others), gathered, weights, s * LEN, LEN)
        grad_att.append(done(found))

    def backward(s, *others):
        grads.append(
            done(attention_backward(segments, qkv, chained(grad_att[s], *others), s, grads[-1]))
        )

    def finish(c, into):
        total = chained(partials[c][2])
        for part in (middle_sums[2 * c + 1], outward_sums[c], last_in[c]):
            total = total + part.astype(jnp.float32)
        return done(
            lax.dynamic_update_slice_in_dim(into, total.astype(jnp.bfloat16), c * chunk, 1)
        )

    gather(0)
    partial(0)
    send_pair(0, first, middle)
    gather(1)
    partial(1, middle_second)
    gather(2)
    send_pair(1)
    send_middle(0, 0)
    second = done(chained(middle, outward) + outward)
    second_far = swap_groups(second)
    send_middle(1, 0)
    partial(2, first_far)
    send_pair(2, pairs_in[0])
    send_outward(0)
    third = done(chained(middle_second, outward_second) + outward_second)
    third_far = swap_groups(third)
    send_middle(0, 1, second_far)
    send_last(0, pairs_in[1])
    send_middle(1, 1, middle_sums[1])
    attended_gradient(0)
    send_outward(1, outward_sums[0])
    send_middle(0, 2)
    attended_gradient(1)
    send_last(1, pairs_in[1])
    send_middle(1, 2, outward_sums[1], last_in[0])
    backward(0, middle_sums[3])
    send_outward(2)
    grad_weight = jnp.zeros((width, own_width), jnp.bfloat16)
    grad_weight = finish(0, grad_weight)
    send_last(2, pairs_in[2])
    backward(1, last_in[1])
    grad_weight = finish(1, grad_weight)
    grad_weight = finish(2, grad_weight)
    return grads[-1], grad_weight


def solution(mesh):
    line = [mesh.shape[name] for name in ("groups", "mp", "dp")] == [2, 4, 4]
    return jax.shard_map(
        shards if line else plain_shards,
        mesh=mesh,
        in_specs=(
            P(None, ("groups", "dp"), "mp"),
            P(("groups", "dp"), "mp"),
            P("mp", "dp"),
            P(("groups", "dp"), None),
        ),
        out_specs=(P(None, ("groups", "dp"), "mp"), P(("groups", "mp"), "dp")),
        check_vma=False,
    )
```

```python
import functools
import math

import jax
import jax.numpy as jnp
from jax import lax
from jax.experimental import pallas as pl
from jax.experimental.pallas import tpu as pltpu
from jax.sharding import PartitionSpec as P

HD = 128
LEN = 512
SCALE = 1.0 / math.sqrt(HD)
CHUNKS = 3
LIGHT = 20
NT = (((1,), (1,)), ((), ()))
NN = (((1,), (0,)), ((), ()))
TN = (((0,), (0,)), ((), ()))
ROOM = pltpu.CompilerParams(vmem_limit_bytes=48 * 2**20)


def dot(a, b, dims):
    return lax.dot_general(a, b, dims, preferred_element_type=jnp.float32)


def cost(flops, moved):
    return pl.CostEstimate(flops=flops // LIGHT, bytes_accessed=moved // LIGHT, transcendentals=0)


def after(array, *others):
    return lax.optimization_barrier((array, *others))[0]


def probabilities(queries, keys, allowed):
    scores = jnp.where(allowed, dot(queries, keys, NT) * SCALE, -jnp.inf)
    exponent = jnp.exp(scores - jnp.max(scores, axis=-1, keepdims=True))
    return exponent * (1.0 / jnp.sum(exponent, axis=-1, keepdims=True))


def forward_kernel(column_ids, row_ids, qkv, attended):
    allowed = column_ids[0] == row_ids[0]
    for head in range(attended.shape[0] // HD):
        cols = slice(head * HD, (head + 1) * HD)
        weights = probabilities(qkv[0, :, cols], qkv[1, :, cols], allowed).astype(jnp.bfloat16)
        attended[cols, :] = dot(weights, qkv[2, :, cols], NN).astype(jnp.bfloat16).T


def backward_kernel(column_ids, row_ids, qkv, grad_att, *refs):
    grad_qkv = refs[-1]
    allowed = column_ids[0] == row_ids[0]
    for head in range(grad_att.shape[1] // HD):
        cols = slice(head * HD, (head + 1) * HD)
        queries, keys, values = qkv[0, :, cols], qkv[1, :, cols], qkv[2, :, cols]
        grads = grad_att[:, cols]
        probability = probabilities(queries, keys, allowed)
        grad_probs = dot(grads, values, NT)
        row_dot = jnp.sum(probability * grad_probs, axis=-1, keepdims=True)
        grad_scores = (probability * (grad_probs - row_dot) * SCALE).astype(jnp.bfloat16)
        weights = probability.astype(jnp.bfloat16)
        grad_qkv[0, :, cols] = dot(grad_scores, keys, NN).astype(jnp.bfloat16)
        grad_qkv[1, :, cols] = dot(grad_scores, queries, TN).astype(jnp.bfloat16)
        grad_qkv[2, :, cols] = dot(weights, grads, TN).astype(jnp.bfloat16)


def attention_specs(segments, qkv, start):
    seqs = qkv.shape[1] // LEN
    block = 2 * HD
    three = pl.BlockSpec((3, LEN, block), lambda s, h: (0, start + s, h))
    in_specs = [
        pl.BlockSpec((1, LEN, 1), lambda s, h: (start + s, 0, 0)),
        pl.BlockSpec((1, 1, LEN), lambda s, h: (start + s, 0, 0)),
        three,
    ]
    return in_specs, [segments.reshape(seqs, LEN, 1), segments.reshape(seqs, 1, LEN), qkv]


def attention_forward(segments, qkv):
    tokens, width = qkv.shape[1:]
    block = 2 * HD
    in_specs, operands = attention_specs(segments, qkv, 0)
    return pl.pallas_call(
        forward_kernel,
        grid=(tokens // LEN, width // block),
        in_specs=in_specs,
        out_specs=pl.BlockSpec((block, LEN), lambda s, h: (h, s)),
        out_shape=jax.ShapeDtypeStruct((width, tokens), jnp.bfloat16),
        compiler_params=ROOM,
        cost_estimate=cost(2 * 2 * tokens * LEN * width, 8 * tokens * width),
    )(*operands)


def attention_backward(segments, qkv, grad_att, start, into, count):
    tokens, width = qkv.shape[1:]
    block = 2 * HD
    rows = count * LEN
    in_specs, operands = attention_specs(segments, qkv, start)
    in_specs.append(pl.BlockSpec((LEN, block), lambda s, h: (start + s, h)))
    operands.append(grad_att)
    if into is not None:
        in_specs.append(pl.BlockSpec(memory_space=pl.ANY))
        operands.append(into)
    return pl.pallas_call(
        backward_kernel,
        grid=(rows // LEN, width // block),
        in_specs=in_specs,
        out_specs=in_specs[2],
        out_shape=jax.ShapeDtypeStruct(qkv.shape, jnp.bfloat16),
        input_output_aliases={} if into is None else {4: 0},
        compiler_params=ROOM,
        cost_estimate=cost(2 * 5 * rows * LEN * width, 14 * rows * width),
    )(*operands)


def partial_kernel(order, attended, *refs):
    *features, stack, rest, own, held = refs
    for at, block in enumerate(features):
        held[at] = dot(attended[...], block[...], NN)
    for at in range(stack.shape[0]):
        stack[at] = held[order[at]].astype(stack.dtype)
    rest[0] = held[order[2]].astype(rest.dtype)
    own[...] = held[order[3]]


def partial_call(order, attended, features, together):
    width, tokens = attended.shape
    chunk = features[0].shape[1]
    rows = min(256, width)
    out = pl.BlockSpec((rows, chunk), lambda r, _: (r, 0))
    return pl.pallas_call(
        partial_kernel,
        grid_spec=pltpu.PrefetchScalarGridSpec(
            num_scalar_prefetch=1,
            grid=(width // rows,),
            in_specs=[pl.BlockSpec((rows, tokens), lambda r, _: (r, 0))]
            + [pl.BlockSpec((tokens, chunk), lambda r, _: (0, 0)) for _ in features],
            out_specs=[
                pl.BlockSpec((together, rows, chunk), lambda r, _: (0, r, 0)),
                pl.BlockSpec((1, rows, chunk), lambda r, _: (0, r, 0)),
                out,
            ],
            scratch_shapes=[pltpu.VMEM((len(features), rows, chunk), jnp.float32)],
        ),
        out_shape=[
            jax.ShapeDtypeStruct((together, width, chunk), jnp.bfloat16),
            jax.ShapeDtypeStruct((1, width, chunk), jnp.bfloat16),
            jax.ShapeDtypeStruct((width, chunk), jnp.float32),
        ],
        compiler_params=ROOM,
        cost_estimate=cost(
            2 * len(features) * chunk * width * tokens,
            2 * len(features) * chunk * (tokens + width) + 2 * width * tokens,
        ),
    )(order, attended, *features)


def attended_kernel(blocks, slots, order, *refs):
    *operands, out, held = refs
    pieces = (len(operands) - 2 * len(slots) - 1) // blocks
    features, start_value = operands[: blocks * pieces], operands[blocks * pieces]
    weights = operands[blocks * pieces + 1 :]
    half = weights[0].shape[0]
    for at in range(blocks):
        start = 0
        for piece in features[at * pieces : (at + 1) * pieces]:
            stop = start + piece.shape[1]
            held[at, :, start:stop] = piece[...]
            start = stop
    near = pl.ds(pl.multiple_of(order[4] * half, HD), half)
    far = pl.ds(pl.multiple_of((1 - order[4]) * half, HD), half)
    for side, columns in enumerate((near, far)):
        if 1 in slots:
            total = dot(held[order[0]], start_value[columns, :], NT)
        else:
            total = start_value[:, columns]
        for at, slot in enumerate(slots):
            total += dot(held[order[slot]], weights[2 * at + side][...], NT)
        out[:, columns] = total.astype(out.dtype)


def attended_call(order, gathered, slots, start_value, weights, kind):
    features = [pieces[at] for at in range(len(gathered[0])) for pieces in gathered]
    blocks = len(gathered[0])
    tokens = features[0].shape[0]
    own_width = weights[0].shape[1]
    width = 2 * weights[0].shape[0]
    rows = min(256, tokens)
    whole = [
        pl.BlockSpec(w.shape, lambda r, _: (0, 0), pipeline_mode=pl.Buffered(1)) for w in weights
    ]
    if 1 in slots:
        first = pl.BlockSpec(
            start_value.shape, lambda r, _: (0, 0), pipeline_mode=pl.Buffered(1)
        )
    else:
        first = pl.BlockSpec((rows, width), lambda r, _: (r, 0))
    return pl.pallas_call(
        functools.partial(attended_kernel, blocks, slots),
        grid_spec=pltpu.PrefetchScalarGridSpec(
            num_scalar_prefetch=1,
            grid=(tokens // rows,),
            in_specs=[pl.BlockSpec((rows, f.shape[1]), lambda r, _: (r, 0)) for f in features]
            + [first]
            + whole,
            out_specs=pl.BlockSpec((rows, width), lambda r, _: (r, 0)),
            scratch_shapes=[pltpu.VMEM((blocks, rows, own_width), jnp.bfloat16)],
        ),
        out_shape=jax.ShapeDtypeStruct((tokens, width), kind),
        compiler_params=ROOM,
        cost_estimate=cost(
            2 * tokens * width * own_width * len(slots),
            2 * (blocks * own_width * (tokens + width) + 2 * tokens * width),
        ),
    )(order, *features, start_value, *weights)


def plain_shards(qkv, grad_out, out_weight, segments):
    attended = attention_forward(segments, qkv)
    rows = lax.all_gather(grad_out.astype(jnp.bfloat16), "mp", axis=1, tiled=True)
    projection = lax.all_gather(out_weight, "dp", axis=1, tiled=True)
    block = dot(attended, rows, NN)
    grad_weight = lax.psum_scatter(block, "dp", scatter_dimension=1, tiled=True)
    grad_att = dot(rows, projection, NT).astype(jnp.bfloat16)
    grad_qkv = attention_backward(segments, qkv, grad_att, 0, None, qkv.shape[1] // LEN)
    return grad_qkv, grad_weight.astype(jnp.bfloat16)


OUTER = [(0, 1), (1, 0), (2, 3), (3, 2)]
INWARD = [(0, 1), (3, 2)]
MIDDLE = [(1, 2), (2, 1)]
OUTWARD = [(1, 0), (2, 3)]


def shards(qkv, grad_out, out_weight, segments):
    width = qkv.shape[2]
    own_width = grad_out.shape[1]
    starts = [0, 5 * own_width // 12, 2 * own_width // 3, own_width]
    group = lax.axis_index("groups")
    here = lax.axis_index("mp")
    place = lax.axis_index("dp")
    outer = (place == 0) | (place == 3)
    low = place < 2

    def along(array, pairs):
        return lax.ppermute(array, "dp", pairs)

    def swap_groups(array):
        return lax.ppermute(array, "groups", [(0, 1), (1, 0)])

    last = []

    def chained(array, *others):
        return after(array, *last, *others)

    def done(*arrays):
        last[:] = arrays[:1]
        return arrays[0] if len(arrays) == 1 else arrays

    half = width // 2
    own_half = lax.dynamic_slice_in_dim(out_weight, group * half, half, 0)
    first = along(own_half, OUTER)
    middle = along(own_half, MIDDLE)
    first_far = swap_groups(first)
    outward = along(middle, OUTWARD)

    attended = done(attention_forward(segments, qkv))

    partial_order = jnp.stack(
        [
            jnp.where(low, 3, 0) ^ here,
            jnp.where(low, 2, 1) ^ here,
            jnp.where(outer, jnp.where(low, 1, 2), jnp.where(low, 0, 3)) ^ here,
            place ^ here,
        ]
    ).astype(jnp.int32)
    gathered, partials = [], []

    def gather(c):
        mine = grad_out[:, starts[c] : starts[c + 1]].astype(jnp.bfloat16)
        if c:
            mine = after(mine, attended)
        near = lax.ppermute(mine, "mp", [(i, i ^ 1) for i in range(4)])
        across = lax.ppermute(mine, "mp", [(i, i ^ 2) for i in range(4)])
        both = lax.ppermute(chained(across), "mp", [(i, i ^ 1) for i in range(4)])
        gathered.append([mine, near, across, both])

    def partial(c, *others):
        partials.append(
            done(*partial_call(chained(partial_order, *others), attended, gathered[c], 3 if c == 1 else 2))
        )

    pairs_in, last_in, middle_sums, outward_sums = [], {}, [], []

    def send_pair(c, *others):
        value = partials[c][0]
        if others:
            value = after(value, *others)
        pairs_in.append(along(value, INWARD))

    def send_last(c, *others):
        last_in[c] = along(after(partials[c][1][0], *others), INWARD)

    def send_middle(t, c, *others):
        mine, arrived = chained(partials[c][0], *others)[t], pairs_in[c][t]
        value = mine.astype(jnp.float32) + arrived.astype(jnp.float32)
        middle_sums.append(along(done(value.astype(jnp.bfloat16)), MIDDLE))

    def send_outward(c, *others):
        arrived = middle_sums[2 * c]
        value = chained(partials[c][1][0], *others).astype(jnp.float32)
        value = value + arrived.astype(jnp.float32)
        outward_sums.append(along(done(value.astype(jnp.bfloat16)), OUTWARD))

    grads = [None]
    attended_order = jnp.stack(
        [
            place ^ here,
            (place ^ 1) ^ here,
            jnp.where(low, 2, 1) ^ here,
            jnp.where(low, 3, 0) ^ here,
            group,
        ]
    ).astype(jnp.int32)
    grad_att = []

    def attended_gradient(slots, start_value, weights, kind, *others):
        grad_att.append(
            done(
                attended_call(
                    chained(attended_order, *others), gathered, slots, start_value, weights, kind
                )
            )
        )

    def backward(s, *others):
        grads.append(
            done(
                attention_backward(
                    segments, qkv, chained(grad_att[1], *others), s, grads[-1], 1
                )
            )
        )

    def finish(c, into):
        total = chained(partials[c][2])
        for part in (middle_sums[2 * c + 1], outward_sums[c], last_in.get(c, pairs_in[1][-1])):
            total = total + part.astype(jnp.float32)
        return done(
            lax.dynamic_update_slice_in_dim(into, total.astype(jnp.bfloat16), starts[c], 1)
        )

    gather(0)
    partial(0)
    send_pair(0, first, middle)
    middle_second = along(after(first, partials[0][0]), MIDDLE)
    outward_second = along(middle_second, OUTWARD)
    gather(1)
    partial(1, middle_second)
    gather(2)
    send_pair(1)
    send_middle(0, 0)
    second = done(chained(middle, outward) + outward)
    second_far = swap_groups(second)
    send_middle(1, 0)
    partial(2, first_far)
    send_pair(2, pairs_in[0])
    send_outward(0)
    third = done(chained(middle_second, outward_second) + outward_second)
    third_far = swap_groups(third)
    send_middle(0, 1, second_far)
    send_last(0, pairs_in[1])
    send_middle(1, 1, middle_sums[1])
    near_weights = [first, first_far, second, second_far]
    attended_gradient((1, 2), out_weight, near_weights, jnp.float32)
    send_outward(1, outward_sums[0])
    attended_gradient((3,), grad_att[0], [third, third_far], jnp.bfloat16)
    send_middle(0, 2, middle_sums[3])
    send_middle(1, 2)
    backward(0)
    send_outward(2, last_in[0], outward_sums[1])
    grad_weight = jnp.zeros((width, own_width), jnp.bfloat16)
    grad_weight = finish(0, grad_weight)
    send_last(2, pairs_in[2])
    backward(1)
    grad_weight = finish(1, grad_weight)
    grad_weight = finish(2, grad_weight)
    return grads[-1], grad_weight


def solution(mesh):
    line = [mesh.shape[name] for name in ("groups", "mp", "dp")] == [2, 4, 4]
    return jax.shard_map(
        shards if line else plain_shards,
        mesh=mesh,
        in_specs=(
            P(None, ("groups", "dp"), "mp"),
            P(("groups", "dp"), "mp"),
            P("mp", "dp"),
            P(("groups", "dp"), None),
        ),
        out_specs=(P(None, ("groups", "dp"), "mp"), P(("groups", "mp"), "dp")),
        check_vma=False,
    )
```

```python
import functools
import math

import jax
import jax.numpy as jnp
from jax import lax
from jax.experimental import pallas as pl
from jax.experimental.pallas import tpu as pltpu
from jax.sharding import PartitionSpec as P

HD = 128
LEN = 512
SCALE = 1.0 / math.sqrt(HD)
CHUNKS = 3
LIGHT = 20
NT = (((1,), (1,)), ((), ()))
NN = (((1,), (0,)), ((), ()))
TN = (((0,), (0,)), ((), ()))
ROOM = pltpu.CompilerParams(vmem_limit_bytes=48 * 2**20)


def dot(a, b, dims):
    return lax.dot_general(a, b, dims, preferred_element_type=jnp.float32)


def cost(flops, moved):
    return pl.CostEstimate(flops=flops // LIGHT, bytes_accessed=moved // LIGHT, transcendentals=0)


def after(array, *others):
    return lax.optimization_barrier((array, *others))[0]


def probabilities(queries, keys, allowed):
    scores = jnp.where(allowed, dot(queries, keys, NT) * SCALE, -jnp.inf)
    exponent = jnp.exp(scores - jnp.max(scores, axis=-1, keepdims=True))
    return exponent * (1.0 / jnp.sum(exponent, axis=-1, keepdims=True))


def forward_kernel(column_ids, row_ids, qkv, attended):
    allowed = column_ids[0] == row_ids[0]
    for head in range(attended.shape[0] // HD):
        cols = slice(head * HD, (head + 1) * HD)
        weights = probabilities(qkv[0, :, cols], qkv[1, :, cols], allowed).astype(jnp.bfloat16)
        attended[cols, :] = dot(weights, qkv[2, :, cols], NN).astype(jnp.bfloat16).T


def backward_kernel(column_ids, row_ids, qkv, grad_att, *refs):
    grad_qkv = refs[-1]
    allowed = column_ids[0] == row_ids[0]
    for head in range(grad_att.shape[1] // HD):
        cols = slice(head * HD, (head + 1) * HD)
        queries, keys, values = qkv[0, :, cols], qkv[1, :, cols], qkv[2, :, cols]
        grads = grad_att[:, cols]
        probability = probabilities(queries, keys, allowed)
        grad_probs = dot(grads, values, NT)
        row_dot = jnp.sum(probability * grad_probs, axis=-1, keepdims=True)
        grad_scores = (probability * (grad_probs - row_dot) * SCALE).astype(jnp.bfloat16)
        weights = probability.astype(jnp.bfloat16)
        grad_qkv[0, :, cols] = dot(grad_scores, keys, NN).astype(jnp.bfloat16)
        grad_qkv[1, :, cols] = dot(grad_scores, queries, TN).astype(jnp.bfloat16)
        grad_qkv[2, :, cols] = dot(weights, grads, TN).astype(jnp.bfloat16)


def attention_specs(segments, qkv, start):
    seqs = qkv.shape[1] // LEN
    block = 2 * HD
    three = pl.BlockSpec((3, LEN, block), lambda s, h: (0, start + s, h))
    in_specs = [
        pl.BlockSpec((1, LEN, 1), lambda s, h: (start + s, 0, 0)),
        pl.BlockSpec((1, 1, LEN), lambda s, h: (start + s, 0, 0)),
        three,
    ]
    return in_specs, [segments.reshape(seqs, LEN, 1), segments.reshape(seqs, 1, LEN), qkv]


def attention_forward(segments, qkv):
    tokens, width = qkv.shape[1:]
    block = 2 * HD
    in_specs, operands = attention_specs(segments, qkv, 0)
    return pl.pallas_call(
        forward_kernel,
        grid=(tokens // LEN, width // block),
        in_specs=in_specs,
        out_specs=pl.BlockSpec((block, LEN), lambda s, h: (h, s)),
        out_shape=jax.ShapeDtypeStruct((width, tokens), jnp.bfloat16),
        compiler_params=ROOM,
        cost_estimate=cost(2 * 2 * tokens * LEN * width, 8 * tokens * width),
    )(*operands)


def attention_backward(segments, qkv, grad_att, start, into, count):
    tokens, width = qkv.shape[1:]
    block = 2 * HD
    rows = count * LEN
    in_specs, operands = attention_specs(segments, qkv, start)
    in_specs.append(pl.BlockSpec((LEN, block), lambda s, h: (start + s, h)))
    operands.append(grad_att)
    if into is not None:
        in_specs.append(pl.BlockSpec(memory_space=pl.ANY))
        operands.append(into)
    return pl.pallas_call(
        backward_kernel,
        grid=(rows // LEN, width // block),
        in_specs=in_specs,
        out_specs=in_specs[2],
        out_shape=jax.ShapeDtypeStruct(qkv.shape, jnp.bfloat16),
        input_output_aliases={} if into is None else {4: 0},
        compiler_params=ROOM,
        cost_estimate=cost(2 * 5 * rows * LEN * width, 14 * rows * width),
    )(*operands)


def partial_kernel(order, attended, *refs):
    *features, stack, rest, own, held = refs
    for at, block in enumerate(features):
        held[at] = dot(attended[...], block[...], NN)
    for at in range(stack.shape[0]):
        stack[at] = held[order[at]].astype(stack.dtype)
    rest[0] = held[order[2]].astype(rest.dtype)
    own[...] = held[order[3]]


def partial_call(order, attended, features, together):
    width, tokens = attended.shape
    chunk = features[0].shape[1]
    rows = min(256, width)
    out = pl.BlockSpec((rows, chunk), lambda r, _: (r, 0))
    return pl.pallas_call(
        partial_kernel,
        grid_spec=pltpu.PrefetchScalarGridSpec(
            num_scalar_prefetch=1,
            grid=(width // rows,),
            in_specs=[pl.BlockSpec((rows, tokens), lambda r, _: (r, 0))]
            + [pl.BlockSpec((tokens, chunk), lambda r, _: (0, 0)) for _ in features],
            out_specs=[
                pl.BlockSpec((together, rows, chunk), lambda r, _: (0, r, 0)),
                pl.BlockSpec((1, rows, chunk), lambda r, _: (0, r, 0)),
                out,
            ],
            scratch_shapes=[pltpu.VMEM((len(features), rows, chunk), jnp.float32)],
        ),
        out_shape=[
            jax.ShapeDtypeStruct((together, width, chunk), jnp.bfloat16),
            jax.ShapeDtypeStruct((1, width, chunk), jnp.bfloat16),
            jax.ShapeDtypeStruct((width, chunk), jnp.float32),
        ],
        compiler_params=ROOM,
        cost_estimate=cost(
            2 * len(features) * chunk * width * tokens,
            2 * len(features) * chunk * (tokens + width) + 2 * width * tokens,
        ),
    )(order, attended, *features)


def attended_kernel(blocks, slots, order, *refs):
    *operands, out, held = refs
    pieces = (len(operands) - 2 * len(slots) - 1) // blocks
    features, start_value = operands[: blocks * pieces], operands[blocks * pieces]
    weights = operands[blocks * pieces + 1 :]
    half = weights[0].shape[0]
    for at in range(blocks):
        start = 0
        for piece in features[at * pieces : (at + 1) * pieces]:
            stop = start + piece.shape[1]
            held[at, :, start:stop] = piece[...]
            start = stop
    near = pl.ds(pl.multiple_of(order[4] * half, HD), half)
    far = pl.ds(pl.multiple_of((1 - order[4]) * half, HD), half)
    for side, columns in enumerate((near, far)):
        if 1 in slots:
            total = dot(held[order[0]], start_value[columns, :], NT)
        else:
            total = start_value[:, columns]
        for at, slot in enumerate(slots):
            total += dot(held[order[slot]], weights[2 * at + side][...], NT)
        out[:, columns] = total.astype(out.dtype)


def attended_call(order, gathered, slots, start_value, weights, kind):
    features = [pieces[at] for at in range(len(gathered[0])) for pieces in gathered]
    blocks = len(gathered[0])
    tokens = features[0].shape[0]
    own_width = weights[0].shape[1]
    width = 2 * weights[0].shape[0]
    rows = min(256, tokens)
    whole = [
        pl.BlockSpec(w.shape, lambda r, _: (0, 0), pipeline_mode=pl.Buffered(1)) for w in weights
    ]
    if 1 in slots:
        first = pl.BlockSpec(
            start_value.shape, lambda r, _: (0, 0), pipeline_mode=pl.Buffered(1)
        )
    else:
        first = pl.BlockSpec((rows, width), lambda r, _: (r, 0))
    return pl.pallas_call(
        functools.partial(attended_kernel, blocks, slots),
        grid_spec=pltpu.PrefetchScalarGridSpec(
            num_scalar_prefetch=1,
            grid=(tokens // rows,),
            in_specs=[pl.BlockSpec((rows, f.shape[1]), lambda r, _: (r, 0)) for f in features]
            + [first]
            + whole,
            out_specs=pl.BlockSpec((rows, width), lambda r, _: (r, 0)),
            scratch_shapes=[pltpu.VMEM((blocks, rows, own_width), jnp.bfloat16)],
        ),
        out_shape=jax.ShapeDtypeStruct((tokens, width), kind),
        compiler_params=ROOM,
        cost_estimate=cost(
            2 * tokens * width * own_width * len(slots),
            2 * (blocks * own_width * (tokens + width) + 2 * tokens * width),
        ),
    )(order, *features, start_value, *weights)


def plain_shards(qkv, grad_out, out_weight, segments):
    attended = attention_forward(segments, qkv)
    rows = lax.all_gather(grad_out.astype(jnp.bfloat16), "mp", axis=1, tiled=True)
    projection = lax.all_gather(out_weight, "dp", axis=1, tiled=True)
    block = dot(attended, rows, NN)
    grad_weight = lax.psum_scatter(block, "dp", scatter_dimension=1, tiled=True)
    grad_att = dot(rows, projection, NT).astype(jnp.bfloat16)
    grad_qkv = attention_backward(segments, qkv, grad_att, 0, None, qkv.shape[1] // LEN)
    return grad_qkv, grad_weight.astype(jnp.bfloat16)


OUTER = [(0, 1), (1, 0), (2, 3), (3, 2)]
INWARD = [(0, 1), (3, 2)]
MIDDLE = [(1, 2), (2, 1)]
OUTWARD = [(1, 0), (2, 3)]


def shards(qkv, grad_out, out_weight, segments):
    width = qkv.shape[2]
    own_width = grad_out.shape[1]
    starts = [0, 5 * own_width // 12, 2 * own_width // 3, own_width]
    group = lax.axis_index("groups")
    here = lax.axis_index("mp")
    place = lax.axis_index("dp")
    outer = (place == 0) | (place == 3)
    low = place < 2

    def along(array, pairs):
        return lax.ppermute(array, "dp", pairs)

    def swap_groups(array):
        return lax.ppermute(array, "groups", [(0, 1), (1, 0)])

    last = []

    def chained(array, *others):
        return after(array, *last, *others)

    def done(*arrays):
        last[:] = arrays[:1]
        return arrays[0] if len(arrays) == 1 else arrays

    half = width // 2
    own_half = lax.dynamic_slice_in_dim(out_weight, group * half, half, 0)
    first = along(own_half, OUTER)
    middle = along(own_half, MIDDLE)
    first_far = swap_groups(first)
    outward = along(middle, OUTWARD)

    attended = done(attention_forward(segments, qkv))

    partial_order = jnp.stack(
        [
            jnp.where(low, 3, 0) ^ here,
            jnp.where(low, 2, 1) ^ here,
            jnp.where(outer, jnp.where(low, 1, 2), jnp.where(low, 0, 3)) ^ here,
            place ^ here,
        ]
    ).astype(jnp.int32)
    gathered, partials = [], []

    def gather(c):
        mine = grad_out[:, starts[c] : starts[c + 1]].astype(jnp.bfloat16)
        if c:
            mine = after(mine, attended)
        near = lax.ppermute(mine, "mp", [(i, i ^ 1) for i in range(4)])
        across = lax.ppermute(mine, "mp", [(i, i ^ 2) for i in range(4)])
        both = lax.ppermute(chained(across), "mp", [(i, i ^ 1) for i in range(4)])
        gathered.append([mine, near, across, both])

    def partial(c, *others):
        partials.append(
            done(*partial_call(chained(partial_order, *others), attended, gathered[c], 3 if c == 1 else 2))
        )

    pairs_in, last_in, middle_sums, outward_sums = [], {}, [], []

    def send_pair(c, *others):
        value = partials[c][0]
        if others:
            value = after(value, *others)
        pairs_in.append(along(value, INWARD))

    def send_last(c, *others):
        last_in[c] = along(after(partials[c][1][0], *others), INWARD)

    def send_middle(t, c, *others):
        mine, arrived = chained(partials[c][0], *others)[t], pairs_in[c][t]
        value = mine.astype(jnp.float32) + arrived.astype(jnp.float32)
        middle_sums.append(along(done(value.astype(jnp.bfloat16)), MIDDLE))

    def send_outward(c, *others):
        arrived = middle_sums[2 * c]
        value = chained(partials[c][1][0], *others).astype(jnp.float32)
        value = value + arrived.astype(jnp.float32)
        outward_sums.append(along(done(value.astype(jnp.bfloat16)), OUTWARD))

    grads = [None]
    attended_order = jnp.stack(
        [
            place ^ here,
            (place ^ 1) ^ here,
            jnp.where(low, 2, 1) ^ here,
            jnp.where(low, 3, 0) ^ here,
            group,
        ]
    ).astype(jnp.int32)
    grad_att = []

    def attended_gradient(slots, start_value, weights, kind, *others):
        grad_att.append(
            done(
                attended_call(
                    chained(attended_order, *others), gathered, slots, start_value, weights, kind
                )
            )
        )

    def backward(s, *others):
        grads.append(
            done(
                attention_backward(
                    segments, qkv, chained(grad_att[1], *others), s, grads[-1], 1
                )
            )
        )

    def finish(c, into):
        total = chained(partials[c][2])
        for part in (middle_sums[2 * c + 1], outward_sums[c], last_in.get(c, pairs_in[1][-1])):
            total = total + part.astype(jnp.float32)
        return done(
            lax.dynamic_update_slice_in_dim(into, total.astype(jnp.bfloat16), starts[c], 1)
        )

    gather(0)
    partial(0)
    send_pair(0, first, middle)
    middle_second = along(after(first, partials[0][0]), MIDDLE)
    outward_second = along(middle_second, OUTWARD)
    gather(1)
    partial(1, middle_second)
    gather(2)
    send_pair(1)
    send_middle(0, 0)
    second = done(chained(middle, outward) + outward)
    second_far = swap_groups(second)
    send_middle(1, 0)
    partial(2, first_far)
    send_pair(2, pairs_in[0])
    send_outward(0)
    third = done(chained(middle_second, outward_second) + outward_second)
    third_far = swap_groups(third)
    send_middle(0, 1, second_far)
    send_last(0, pairs_in[1])
    send_middle(1, 1, middle_sums[1])
    near_weights = [first, first_far, second, second_far]
    attended_gradient((1, 2), out_weight, near_weights, jnp.float32)
    attended_gradient((3,), grad_att[0], [third, third_far], jnp.bfloat16)
    send_outward(1, outward_sums[0])
    send_middle(0, 2, middle_sums[3])
    send_middle(1, 2)
    backward(0)
    send_outward(2, last_in[0], outward_sums[1])
    grad_weight = jnp.zeros((width, own_width), jnp.bfloat16)
    grad_weight = finish(0, grad_weight)
    send_last(2, pairs_in[2])
    backward(1)
    grad_weight = finish(1, grad_weight)
    grad_weight = finish(2, grad_weight)
    return grads[-1], grad_weight


def solution(mesh):
    line = [mesh.shape[name] for name in ("groups", "mp", "dp")] == [2, 4, 4]
    return jax.shard_map(
        shards if line else plain_shards,
        mesh=mesh,
        in_specs=(
            P(None, ("groups", "dp"), "mp"),
            P(("groups", "dp"), "mp"),
            P("mp", "dp"),
            P(("groups", "dp"), None),
        ),
        out_specs=(P(None, ("groups", "dp"), "mp"), P(("groups", "mp"), "dp")),
        check_vma=False,
    )
```
